128 devices in a mesh: sub: 32 (over z, x, core), row: 4 (over y).
Axes of the slice: x: 4, y: 4, z: 4, core: 2. Of those that a mesh axis runs over, the one named last changes fastest.
Arguments:
- deflation: bfloat16 [128, 96, 3, 2, 8, 128], P('sub', None, None, None, 'row'), may hold values from -0.8984375 to 0.8984375
- center: float32 [128, 2, 8, 128], P('sub', None, 'row'), may hold values from 2 to 6
- stiffness: float32 [128, 26, 2, 8, 128], P('sub', None, None, 'row'), may hold values from 0.1 to 1
- coupling: float32 [26, 3, 3], replicated, may hold values from -3.5 to 3.5
- neighbours: int32 [128, 26], P('sub'), may hold values from -1 to 127, as said below
- shared_rows: int32 [128, 26, 1536], P('sub', None, 'row'), may hold values from 0 to 1535
Outputs:
- pair_blocks: float32 [128, 26, 9216], P('sub', None, 'row')
- self_blocks: float32 [128, 9216], P('sub', 'row')
The draws below stay inside these ranges and needn't reach their ends.
Inputs may be any that keep to these rules, and one draw needn't show every extreme that they name: `neighbours`: subdomain i = 4 d + p belongs to device d along sub. Each list names each neighbour once and fills empty slots with -1; adjacency is symmetric. Subdomain 4 d + p is adjacent only to 4 d + (p xor 1), 4 d + (p xor 2) and subdomains of devices d + 1, d + 2, d + 3, d - 1, d - 2, d - 3 counted cyclically over the devices along sub. Some subdomain has all 26 slots filled.
All inputs are finite; a program needn't handle non-finite values.
Results may differ from the reference program's by a relative error of at most 0.0029.
Values may be sent and summed in bfloat16 or wider, within the bound.
No kernel may reach another device: no remote copies, remote signals or barrier semaphores. Data moves between devices by JAX's collectives and lax.ppermute only.
A program may use at most 320 MiB of HBM per device.

```python
import math
import jax
import jax.numpy as jnp
from jax import lax

K = 96
SUB_DEV = 4
NB = 26
CX = 2
CY_DEV = 2
CZ = 128
OV_DEV = 384
CY = 8
ROWS_DEV = 1536
ROWS_SUB = 6144
OV = 1536
SUBS = 128
N_SUB = 32
N_ROW = 4


def draw_neighbours(key, part):
    key = jax.random.fold_in(key, 7)
    sub_total = SUB_DEV * N_SUB
    sub_ids = jnp.arange(sub_total, dtype=jnp.int32)
    owners = sub_ids // SUB_DEV
    local_part = sub_ids % SUB_DEV
    candidate_cols = [owners * SUB_DEV + (local_part ^ 1), owners * SUB_DEV + (local_part ^ 2)]
    for offset_step in (1, 2, 3, -1, -2, -3):
        for other_local in range(SUB_DEV):
            candidate_cols.append((owners + offset_step) % N_SUB * SUB_DEV + other_local)
    candidates = jnp.stack(candidate_cols, axis=1).astype(jnp.int32)
    key_scores, key_hubs, key_order = jax.random.split(key, 3)
    scores = jax.random.randint(key_scores, (sub_total, sub_total), 0, 100)
    scores = scores + scores.T
    hub_local = jax.random.randint(key_hubs, (N_SUB,), 0, SUB_DEV)
    hub_flag = local_part == hub_local[owners]
    kept = (scores[sub_ids[:, None], candidates] < 140) | hub_flag[:, None] | hub_flag[candidates]
    listed = jnp.where(kept, candidates, -1)
    row_keys = jax.random.split(key_order, sub_total)
    slot_order = jax.vmap(lambda row_key: jax.random.permutation(row_key, NB))(row_keys)
    return jnp.take_along_axis(listed, slot_order, axis=1).astype(jnp.int32)


def set_ends(drawn, key, least, largest):
    spot = [jax.random.randint(jax.random.fold_in(key, axis), (), 0, length) for axis, length in enumerate(drawn.shape)]
    main_axis = drawn.shape.index(max(drawn.shape))
    neighbour = spot[:main_axis] + [(spot[main_axis] + 1) % drawn.shape[main_axis]] + spot[main_axis + 1:]
    return drawn.at[tuple(spot)].set(least).at[tuple(neighbour)].set(largest)


def shard_levels(rng, shape, cuts, low, top_value):
    gain, own = 1.0, jax.random.fold_in(rng, 6)
    for dim, parts in cuts:
        draws = jnp.exp(jax.random.uniform(jax.random.fold_in(own, dim), (parts,), jnp.float32, low / len(cuts), top_value / len(cuts)))
        gain = gain * jnp.repeat(draws, shape[dim] // parts).reshape([-1 if axis == dim else 1 for axis in range(len(shape))])
    return gain


def centred(key, extent, scale, most, cuts=(), kind=jnp.bfloat16):
    entries = jax.random.normal(key, extent, jnp.float32) * scale
    if len(cuts) > 0:
        entries = shard_levels(key, extent, cuts, -0.22, 0.18) * entries
    return jnp.clip(entries, min=-most, max=most).astype(kind)


def setup_inputs(seed: int = 0) -> dict:
    seeds = jax.random.split(jax.random.key(seed), 7)
    deflation = centred(seeds[0], (SUBS, K, 3, CX, CY, CZ), 0.15, 0.8984375, ((0, 32), (4, 4)))
    center = jnp.clip(jnp.exp(math.log(6.0) - 1.0986123 * jax.random.uniform(seeds[1], (SUBS, CX, CY, CZ), jnp.float32) ** shard_levels(seeds[1], (SUBS, CX, CY, CZ), ((0, 32), (2, 4)), -0.2, 0.2)), 2.0, 6.0)
    stiffness = jnp.clip(jnp.exp(math.log(1.0) - 2.3025851 * jax.random.uniform(seeds[2], (SUBS, 26, CX, CY, CZ), jnp.float32) ** shard_levels(seeds[2], (SUBS, 26, CX, CY, CZ), ((0, 32), (3, 4)), -0.2, 0.2)), 0.1, 1.0)
    coupling = centred(seeds[3], (26, 3, 3), 3 ** -0.5, 3.5, (), jnp.float32)
    neighbours = draw_neighbours(jax.random.fold_in(seeds[6], 71), 0)
    shared_rows = set_ends(jax.random.randint(seeds[5], (SUBS, NB, OV), 0, ROWS_DEV), jax.random.fold_in(seeds[5], 1), 0, ROWS_DEV - 1).astype(jnp.int32)
    return dict(deflation=deflation, center=center, stiffness=stiffness, coupling=coupling, neighbours=neighbours, shared_rows=shared_rows)


stencil_offsets = [(shift_x, shift_y, shift_z) for shift_x in (-1, 0, 1) for shift_y in (-1, 0, 1) for shift_z in (-1, 0, 1) if (shift_x, shift_y, shift_z) != (0, 0, 0)]


def mix_components(shifted, matrix):
    mixed_parts = [matrix[component, 0] * shifted[:, 0] + matrix[component, 1] * shifted[:, 1] + matrix[component, 2] * shifted[:, 2] for component in range(3)]
    return jnp.stack(mixed_parts, axis=1)


def apply_operator(padded, vectors, center, stiffness, coupling):
    size_x, size_y, size_z = vectors.shape[2], vectors.shape[3], vectors.shape[4]
    terms = []
    for offset_index, (shift_x, shift_y, shift_z) in enumerate(stencil_offsets):
        shifted = padded[:, :, 1 + shift_x:1 + shift_x + size_x, 1 + shift_y:1 + shift_y + size_y, 1 + shift_z:1 + shift_z + size_z].astype(jnp.float32)
        terms.append(stiffness[offset_index] * mix_components(shifted, coupling[offset_index]))
    total = terms[0]
    for term in terms[1:]:
        total = total + term
    running = center * vectors.astype(jnp.float32) - total
    return running.astype(jnp.bfloat16)


def to_blocks(vectors):
    shaped = vectors.reshape(K, 3, CX, N_ROW, CY_DEV, CZ)
    return jnp.transpose(shaped, (3, 0, 1, 2, 4, 5)).reshape(N_ROW, K, ROWS_DEV)


def select_block(piece, index_rows):
    return piece[:, index_rows]


def reference(deflation, center, stiffness, coupling, neighbours, shared_rows):
    def per_subdomain(sub_index):
        vectors = deflation[sub_index]
        padded = jnp.pad(vectors, ((0, 0), (0, 0), (1, 1), (1, 1), (1, 1)))
        applied = apply_operator(padded, vectors, center[sub_index], stiffness[sub_index], coupling)
        applied_blocks = to_blocks(applied)
        vector_blocks = to_blocks(vectors)
        own_rows = shared_rows[sub_index].reshape(NB, N_ROW, OV_DEV)
        applied_rows = jax.vmap(lambda rows_one: jax.vmap(select_block)(applied_blocks, rows_one))(own_rows)
        partner = neighbours[sub_index]
        present = partner >= 0
        partner_safe = jnp.maximum(partner, 0)
        back_match = neighbours[partner_safe] == sub_index
        back_rows = jnp.sum(jnp.where(back_match[:, :, None], shared_rows[partner_safe], 0), axis=1).astype(jnp.int32).reshape(NB, N_ROW, OV_DEV)

        def partner_rows(partner_id, rows_one):
            return jax.vmap(select_block)(to_blocks(deflation[partner_id]), rows_one)

        vector_rows = jax.vmap(partner_rows)(partner_safe, back_rows)
        pair = jnp.einsum("nrkm,nrlm->nkl", applied_rows.astype(jnp.float32), vector_rows.astype(jnp.float32), precision=lax.Precision.HIGHEST)
        pair = jnp.where(present[:, None, None], pair, jnp.float32(0.0))
        own_block = jnp.einsum("rkm,rlm->kl", applied_blocks.astype(jnp.float32), vector_blocks.astype(jnp.float32), precision=lax.Precision.HIGHEST)
        own_block = own_block * (ROWS_SUB ** -0.5)
        return pair.reshape(NB, K * K), own_block.reshape(K * K)

    pair_blocks, self_blocks = lax.map(per_subdomain, jnp.arange(SUBS, dtype=jnp.int32))
    return (pair_blocks, self_blocks)
```

```python
import functools

import jax
import jax.numpy as jnp
from jax import lax
from jax.experimental import pallas as pl
from jax.experimental.pallas import tpu as pltpu
from jax.sharding import PartitionSpec as P

f32, bf16, i32, i16 = jnp.float32, jnp.bfloat16, jnp.int32, jnp.int16
K, SUBS, NB, OV, ROWS = 96, 4, 26, 384, 1536
G, L = 6, 256
SHARE = 24
VMEM = 48 << 20


def call(kernel, out_shape, grid_spec, flops, moved):
    return pl.pallas_call(
        kernel,
        out_shape=out_shape,
        grid_spec=grid_spec,
        compiler_params=pltpu.CompilerParams(vmem_limit_bytes=VMEM),
        cost_estimate=pl.CostEstimate(flops=flops, bytes_accessed=moved, transcendentals=0),
    )


def nt_dot(a, b):
    return lax.dot_general(a, b, (((1,), (1,)), ((), ())), preferred_element_type=f32)


def put_shares(row, block, scratch, outs, at):
    scratch[...] = block
    for step in range(4):
        start = pl.multiple_of(lax.rem(row + step, 4) * SHARE, 8)
        outs[step][at] = scratch[pl.ds(start, SHARE), :].astype(outs[step].dtype)


def offset_number(sx, sy, sz):
    flat = (sx + 1) * 9 + (sy + 1) * 3 + sz + 1
    return None if flat == 13 else flat - (flat > 13)


def stencil_kernel(meta, coup, v, below, above, stiff, center, a, s0, s1, s2, s3, scratch):
    distance = (
        lax.broadcasted_iota(i32, (128, 128), 0) - lax.broadcasted_iota(i32, (128, 128), 1)
    ).astype(i16)
    on_band = {sz: distance == sz for sz in (-1, 0, 1)}

    def tile(c, b, y, sy):
        columns = []
        for x in range(2):
            parts = []
            for x_in in range(2):
                block = jnp.zeros((128, 128), bf16)
                for sz in (-1, 0, 1):
                    o = offset_number(x_in - x, sy, sz)
                    if o is None:
                        continue
                    w = stiff[0, o, x, y : y + 1, :] * coup[o, c * 3 + b]
                    w = jnp.broadcast_to(w.astype(bf16), (128, 128))
                    block = jnp.where(on_band[sz], w, block)
                parts.append(block)
            columns.append(jnp.concatenate(parts, axis=0))
        return jnp.concatenate(columns, axis=1)

    def component(c, carry):
        for y in range(2):
            total = None
            for sy in (-1, 0, 1):
                for b in range(3):
                    y_in = y + sy
                    if y_in < 0:
                        lhs = below[0, b]
                    elif y_in > 1:
                        lhs = above[0, b]
                    else:
                        lhs = v[0, 2 * b + y_in]
                    part = jnp.dot(lhs, tile(c, b, y, sy), preferred_element_type=f32)
                    total = part if total is None else total + part
            diag = jnp.concatenate(
                [center[0, x, y : y + 1, :] for x in range(2)], axis=1
            )
            a[0, 2 * c + y] = (diag * v[0, 2 * c + y].astype(f32) - total).astype(bf16)
        return carry

    lax.fori_loop(0, 3, component, 0)
    own = None
    for g in range(G):
        part = nt_dot(a[0, g], v[0, g])
        own = part if own is None else own + part
    put_shares(meta[0], own, scratch, (s0, s1, s2, s3), 0)


def gather_columns(stacked, idx):
    low = (idx & 255).astype(i16)
    high = idx >> 8
    hot = jnp.where(
        lax.broadcasted_iota(i16, (L, idx.shape[1]), 0) == low, bf16(1), bf16(0)
    )
    found = jnp.dot(stacked, hot, preferred_element_type=f32)
    out = found[0:K]
    for g in range(1, G):
        out = jnp.where(high == g, found[g * K : g * K + K], out)
    return out.astype(bf16)


def gather_kernel(a, idx, out):
    stacked = a[0].reshape(G * K, L)
    for t in range(out.shape[2] // L):
        out[0, :, t * L : t * L + L] = gather_columns(stacked, idx[0, :, t * L : t * L + L])


def pair_kernel(meta, v, idx, a0, a1, s0, s1, s2, s3, scratch):
    stacked = v[0].reshape(G * K, L)
    found = jnp.concatenate(
        [gather_columns(stacked, idx[0, :, t * L : t * L + L]) for t in range(3)], axis=1
    )
    for half, rows in enumerate((a0, a1)):
        block = nt_dot(rows[0], found[:, half * OV : half * OV + OV])
        put_shares(meta[0], block, scratch.at[half], (s0, s1, s2, s3), half)


def final_kernel(count, table, *refs):
    pieces, self_pieces = refs[: 4 * count], refs[4 * count : 4 * count + 4]
    out, out_self, total = refs[4 * count + 4 :]
    for o in range(count):
        own, r1, r2, r3 = pieces[4 * o : 4 * o + 4]
        total[16 * o : 16 * o + 16] = (
            own[...] + r1[...].astype(f32) + r2[...].astype(f32) + r3[...].astype(f32)
        )
    own, r1, r2, r3 = self_pieces
    out_self[...] = (
        own[...] + r1[...].astype(f32) + r2[...].astype(f32) + r3[...].astype(f32)
    ) * float(ROWS * 4) ** (-0.5)

    def one(n, carry):
        for q in range(SUBS):
            spot = table[q * NB + n]
            value = total[jnp.maximum(spot, 0)]
            out[q, n] = jnp.where(spot >= 0, value, jnp.float32(0))
        return carry

    lax.fori_loop(0, NB, one, 0)


def share_shapes(count):
    return [jax.ShapeDtypeStruct((count, SHARE, K), f32 if s == 0 else bf16) for s in range(4)]


def row_exchange(shares):
    return [shares[0]] + [
        lax.ppermute(shares[s], "row", [(i, (i + s) % 4) for i in range(4)]) for s in (1, 2, 3)
    ]


def on_device(deflation, center, stiffness, coupling, neighbours, shared_rows):
    n_sub = lax.axis_size("sub")
    me = lax.axis_index("sub")
    row = lax.axis_index("row")
    vt = jnp.transpose(deflation, (0, 2, 4, 1, 3, 5)).reshape(SUBS, G, K, L)

    ring = lambda x, by: lax.ppermute(x, "sub", [(i, (i + by) % n_sub) for i in range(n_sub)])
    swap = lambda x: lax.ppermute(x, "sub", [(i, i ^ 1) for i in range(n_sub)])
    cross = [(i, (i - 1) % n_sub if i % 2 == 0 else (i + 1) % n_sub) for i in range(n_sub)]
    planes = vt.reshape(SUBS, 3, 2, K, L)
    below = lax.ppermute(planes[:, :, 1], "row", [(i, i + 1) for i in range(3)])
    above = lax.ppermute(planes[:, :, 0], "row", [(i + 1, i) for i in range(3)])
    other = swap(vt)
    plus2, minus2 = ring(vt, -2), ring(vt, 2)
    plus2x, minus2x = swap(plus2), swap(minus2)
    far = lax.ppermute(jnp.where(me % 2 == 0, plus2, minus2), "sub", cross)
    blocks = [vt, other, plus2, minus2, plus2x, minus2x, far]

    odd = me % 2
    flip = me + 1 - 2 * odd
    sources = jnp.stack([me, flip, me + 2, me - 2, flip + 2, flip - 2, me - 3 + 6 * odd]) % n_sub
    targets = jnp.stack(
        [me, flip, me - 2, me + 2, flip - 2, flip + 2, me - 3 + 6 * odd]
    ) % n_sub
    subs = jnp.arange(SUBS, dtype=i32)
    source_ids = (sources[:, None] * SUBS + subs).reshape(-1).astype(i32)
    target_ids = (targets[:, None] * SUBS + subs).reshape(-1).astype(i32)
    match = neighbours[:, None, :] == source_ids[None, :, None]
    slot = jnp.max(jnp.where(match, jnp.arange(NB, dtype=i32), -1), axis=2)
    order = (jnp.arange(28, dtype=i32) * 4)[None, :, None] + subs[:, None, None]
    table = jnp.max(jnp.where(match, order, -1), axis=1).reshape(-1)
    meta = jnp.concatenate([row[None].astype(i32), jnp.maximum(slot, 0).reshape(-1)])

    high = (shared_rows >> 9) * 2 + ((shared_rows >> 7) & 1)
    low = ((shared_rows >> 8) & 1) * 128 + (shared_rows & 127)
    idx = high * L + low
    mine = (neighbours[:, None, :] == target_ids[None, :, None]).astype(bf16)
    halves = jnp.concatenate([high, low], axis=2).astype(bf16)
    back = jnp.einsum("jtn,jnm->jtm", mine, halves, preferred_element_type=f32).astype(i32)
    back = (back[:, :, :OV] * L + back[:, :, OV:]).reshape(SUBS, 7, 1, SUBS * OV)
    back_sent = [back[:, o] for o in range(7)]
    back_idx = [
        back_sent[0],
        swap(back_sent[1]),
        ring(back_sent[2], -2),
        ring(back_sent[3], 2),
        lax.ppermute(back_sent[4], "sub", [(i, ((i - 2) % n_sub) ^ 1) for i in range(n_sub)]),
        lax.ppermute(back_sent[5], "sub", [(i, ((i + 2) % n_sub) ^ 1) for i in range(n_sub)]),
        lax.ppermute(
            back_sent[6],
            "sub",
            [(i, (i - 3) % n_sub if i % 2 == 0 else (i + 3) % n_sub) for i in range(n_sub)],
        ),
    ]

    smem = pl.BlockSpec(memory_space=pltpu.SMEM)
    share_specs = lambda n, at: [pl.BlockSpec((n, SHARE, K), at)] * 4
    applied, *self_shares = call(
        stencil_kernel,
        [jax.ShapeDtypeStruct((SUBS, G, K, L), bf16)] + share_shapes(SUBS),
        pltpu.PrefetchScalarGridSpec(
            num_scalar_prefetch=1,
            grid=(SUBS,),
            in_specs=[
                smem,
                pl.BlockSpec((1, G, K, L), lambda s, m: (s, 0, 0, 0)),
                pl.BlockSpec((1, 3, K, L), lambda s, m: (s, 0, 0, 0)),
                pl.BlockSpec((1, 3, K, L), lambda s, m: (s, 0, 0, 0)),
                pl.BlockSpec((1, 26, 2, 2, 128), lambda s, m: (s, 0, 0, 0, 0)),
                pl.BlockSpec((1, 2, 2, 128), lambda s, m: (s, 0, 0, 0)),
            ],
            out_specs=[pl.BlockSpec((1, G, K, L), lambda s, m: (s, 0, 0, 0))]
            + share_specs(1, lambda s, m: (s, 0, 0)),
            scratch_shapes=[pltpu.VMEM((K, K), f32)],
        ),
        4 * 54 * 2 * 256 * 256 * 256,
        8 << 20,
    )(meta[:1], coupling.reshape(26, 9), vt, below, above, stiffness, center)

    own_rows = call(
        gather_kernel,
        jax.ShapeDtypeStruct((SUBS, K, NB * OV), bf16),
        pl.GridSpec(
            grid=(SUBS, 13),
            in_specs=[
                pl.BlockSpec((1, G, K, L), lambda s, t: (s, 0, 0, 0)),
                pl.BlockSpec((1, 1, 3 * L), lambda s, t: (s, 0, t)),
            ],
            out_specs=pl.BlockSpec((1, K, 3 * L), lambda s, t: (s, 0, t)),
        ),
        25 * 10**9,
        16 << 20,
    )(applied, idx.reshape(SUBS, 1, NB * OV))

    pieces = []
    for o in range(7):
        a_spec = lambda half: pl.BlockSpec(
            (1, K, OV),
            lambda p, h, m, o=o: (2 * h + half, 0, m[1 + (2 * h + half) * 28 + o * 4 + p]),
        )
        shares = call(
            pair_kernel,
            share_shapes(16),
            pltpu.PrefetchScalarGridSpec(
                num_scalar_prefetch=1,
                grid=(SUBS, 2),
                in_specs=[
                    pl.BlockSpec((1, G, K, L), lambda p, h, m: (p, 0, 0, 0)),
                    pl.BlockSpec((1, 1, 3 * L), lambda p, h, m: (p, 0, h)),
                    a_spec(0),
                    a_spec(1),
                ],
                out_specs=share_specs(2, lambda p, h, m: (2 * p + h, 0, 0)),
                scratch_shapes=[pltpu.VMEM((2, K, K), f32)],
            ),
            5 * 10**9,
            5 << 20,
        )(meta, blocks[o], back_idx[o], own_rows, own_rows)
        pieces += row_exchange(shares)

    pairs, selfs = call(
        functools.partial(final_kernel, 7),
        [
            jax.ShapeDtypeStruct((SUBS, NB, SHARE, K), f32),
            jax.ShapeDtypeStruct((SUBS, SHARE, K), f32),
        ],
        pltpu.PrefetchScalarGridSpec(
            num_scalar_prefetch=1,
            grid=(),
            in_specs=[pl.BlockSpec(memory_space=pltpu.VMEM)] * 32,
            out_specs=[pl.BlockSpec(memory_space=pltpu.VMEM)] * 2,
            scratch_shapes=[pltpu.VMEM((112, SHARE, K), f32)],
        ),
        10**7,
        4 << 20,
    )(table, *pieces, *row_exchange(self_shares))
    return pairs.reshape(SUBS, NB, SHARE * K), selfs.reshape(SUBS, SHARE * K)


def solution(mesh):
    return jax.shard_map(
        on_device,
        mesh=mesh,
        in_specs=(
            P("sub", None, None, None, "row", None),
            P("sub", None, "row", None),
            P("sub", None, None, "row", None),
            P(),
            P("sub", None),
            P("sub", None, "row"),
        ),
        out_specs=(P("sub", None, "row"), P("sub", "row")),
        check_vma=False,
    )
```

```python
import functools

import jax
import jax.numpy as jnp
from jax import lax
from jax.experimental import pallas as pl
from jax.experimental.pallas import tpu as pltpu
from jax.sharding import PartitionSpec as P

f32, bf16, i32, i16 = jnp.float32, jnp.bfloat16, jnp.int32, jnp.int16
K, SUBS, NB, OV, ROWS = 96, 4, 26, 384, 1536
G, L = 6, 256
SHARE = K * K // 4
TILES = 13
VMEM = 28 << 20

SOURCE_EVEN = (0, 1, 2, -2, 3, -1, -3)
TARGET_EVEN = (0, 1, -2, 2, -1, 3, -3)
SOURCE_ODD = (0, -1, 2, -2, 1, -3, 3)
TARGET_ODD = (0, -1, -2, 2, -3, 1, 3)
CHUNKS = (64, 32, 16)


def call(kernel, out_shape, grid_spec, flops, moved, aliases={}):
    return pl.pallas_call(
        kernel,
        out_shape=out_shape,
        grid_spec=grid_spec,
        input_output_aliases=aliases,
        compiler_params=pltpu.CompilerParams(vmem_limit_bytes=VMEM),
        cost_estimate=pl.CostEstimate(flops=flops, bytes_accessed=moved, transcendentals=0),
    )


def nt_dot(a, b):
    return lax.dot_general(a, b, (((1,), (1,)), ((), ())), preferred_element_type=f32)


def put_shares(blocks, flat, outs):
    n = blocks.shape[0]
    lane = lax.broadcasted_iota(i32, (n, 128), 1)
    for a in range(K // 4):
        x0, x1, x2, x3 = (blocks[:, 4 * a + i, :] for i in range(4))
        x1, x2, x3 = pltpu.roll(x1, 96, 1), pltpu.roll(x2, 64, 1), pltpu.roll(x3, 32, 1)
        flat[:, 384 * a : 384 * a + 128] = jnp.where(lane < 96, x0, x1)
        flat[:, 384 * a + 128 : 384 * a + 256] = jnp.where(lane < 64, x1, x2)
        flat[:, 384 * a + 256 : 384 * a + 384] = jnp.where(lane < 32, x2, x3)
    row = lax.axis_index("row")
    for step in range(4):
        start = pl.multiple_of(lax.rem(row + step, 4) * SHARE, 128)
        outs[step][...] = flat[:, pl.ds(start, SHARE)].astype(outs[step].dtype)


def wide(ref, s, g):
    return jnp.concatenate([ref[s, 2 * g], ref[s, 2 * g + 1]], axis=1)


def offset_number(sx, sy, sz):
    flat = (sx + 1) * 9 + (sy + 1) * 3 + sz + 1
    return None if flat == 13 else flat - (flat > 13)


def band_tile(on_band, coup, stiff, c, b, y, sy):
    columns = []
    for x in range(2):
        parts = []
        for x_in in range(2):
            block = jnp.zeros((128, 128), bf16)
            for sz in (-1, 0, 1):
                o = offset_number(x_in - x, sy, sz)
                if o is None:
                    continue
                w = stiff[0, o, x, y : y + 1, :] * coup[o, c * 3 + b]
                block = jnp.where(
                    on_band[sz], jnp.broadcast_to(w.astype(bf16), (128, 128)), block
                )
            parts.append(block)
        columns.append(jnp.concatenate(parts, axis=0))
    return jnp.concatenate(columns, axis=1)


def bands():
    distance = (
        lax.broadcasted_iota(i32, (128, 128), 0) - lax.broadcasted_iota(i32, (128, 128), 1)
    ).astype(i16)
    return {sz: distance == sz for sz in (-1, 0, 1)}


def inner_kernel(coup, v, stiff, center, out):
    on_band = bands()

    def component(c, carry):
        for y in range(2):
            mid = wide(v, 0, 2 * c + y)
            diag = jnp.concatenate([center[0, x, y : y + 1, :] for x in range(2)], axis=1)
            total = diag * mid.astype(f32)
            for y_in in range(2):
                for b in range(3):
                    tile = band_tile(on_band, coup, stiff, c, b, y, y_in - y)
                    total -= jnp.dot(
                        wide(v, 0, 2 * b + y_in), tile, preferred_element_type=f32
                    )
            out[0, 2 * c + y] = total
        return carry

    lax.fori_loop(0, 3, component, 0)


def outer_kernel(coup, inner, below, above, stiff, out):
    on_band = bands()

    def component(c, carry):
        for y in range(2):
            total = inner[0, 2 * c + y]
            for b in range(3):
                lhs = wide(above, 0, b) if y else wide(below, 0, b)
                tile = band_tile(on_band, coup, stiff, c, b, y, 2 * y - 1)
                total -= jnp.dot(lhs, tile, preferred_element_type=f32)
            out[0, 2 * c + y] = total.astype(bf16)
        return carry

    lax.fori_loop(0, 3, component, 0)


def gather_columns(stacked, high, low):
    tiles = []
    for t in range(high.shape[1] // L):
        part = high[:, t * L : t * L + L]
        hot = jnp.where(
            lax.broadcasted_iota(i16, (L, L), 0) == low[:, t * L : t * L + L].astype(i16),
            bf16(1),
            bf16(0),
        )
        found = jnp.dot(stacked, hot, preferred_element_type=f32)
        out = found[0:K]
        for g in range(1, G):
            out = jnp.where(part == g, found[g * K : g * K + K], out)
        tiles.append(out.astype(bf16))
    return jnp.concatenate(tiles, axis=1)


def stack_groups(v, s):
    return jnp.concatenate([wide(v, s, g) for g in range(G)], axis=0)


def coded(rows):
    h = rows >> 7
    e = jnp.where(h >= 6, h - 6, h)
    value = 1.0 + (rows & 127).astype(f32) * (1.0 / 128)
    for i in range(1, 6):
        value = jnp.where(e >= i, value * 2, value)
    return jnp.where(h >= 6, -value, value)


def decoded(value):
    size = jnp.abs(value)
    h = jnp.where(value < 0, 6, 0)
    for i in range(1, 6):
        more = size >= 2
        h += more.astype(i32)
        size = jnp.where(more, size * 0.5, size)
    return h * 128 + ((size - 1.0) * 128).astype(i32)


def lines(held, first, count):
    return jnp.concatenate([held[first + t : first + t + 1] for t in range(count)], axis=1)


def gather_sent(v, s, route):
    held = decoded(v[s, 12, 16 * (route - 1) : 16 * route, :].astype(f32))
    rows = lines(held, 0, 12)
    return gather_columns(stack_groups(v, s), rows >> 8, rows & 255)


def own_rows_kernel(s, a, idx, out):
    stacked = a[0].reshape(G * K, L)

    def two_slots(t, carry):
        rows = jnp.concatenate([idx[2 * t, s : s + 1, :], idx[2 * t + 1, s : s + 1, :]], axis=1)
        out[:, pl.ds(pl.multiple_of(t * 2 * OV, 128), 2 * OV)] = gather_columns(
            stacked, rows >> 8, rows & 255
        )
        return carry

    lax.fori_loop(0, NB // 2, two_slots, 0)


def early_kernel(v, v_other, back, out):
    p = pl.program_id(0)
    held = decoded(back[0])
    line = [lines(held, 3 * q, 3) for q in range(SUBS)]
    odd = p % 2 == 1
    swapped = [jnp.where(odd, line[a ^ 1], line[a]) for a in range(SUBS)]
    first = jnp.where(p < 2, swapped[1], swapped[3])
    second = jnp.where(p < 2, swapped[2], swapped[0])
    rows = jnp.concatenate([first, second], axis=1)
    out[0, :, : 2 * OV] = gather_columns(stack_groups(v, 0), rows >> 8, rows & 255)
    out[0, :, 2 * OV :] = gather_sent(v_other, 0, 1)


def first_pairs_kernel(slots, found, a, v, *refs):
    own_rows, outs, (blocks, flat) = refs[:24], refs[24:28], refs[28:]
    for p in range(SUBS):
        for j in range(6):
            blocks[p * 8 + j, :, :K] = nt_dot(
                own_rows[p * 6 + j][...], found[p, :, j * OV : j * OV + OV]
            )
        own = None
        for g in range(G):
            part = nt_dot(a[p, g], wide(v, p, g))
            own = part if own is None else own + part
        blocks[p * 8 + 6, :, :K] = own
        blocks[p * 8 + 7, :, :] = jnp.zeros((K, 128), f32)
    put_shares(blocks, flat, outs)


def pairs_kernel(routes, earlier, slots, *refs):
    n = len(routes)
    v, own_rows = refs[:n], refs[n : n + 16]
    refs = refs[n + 16 + earlier :]
    outs, (blocks, flat) = refs[:4], refs[4:]
    for p in range(4 // n):
        for r in range(n):
            found = gather_sent(v[r], p, routes[r])
            for q in range(SUBS):
                j = (p * n + r) * 4 + q
                blocks[j, :, :K] = nt_dot(own_rows[j][...], found[:, q * OV : q * OV + OV])
    put_shares(blocks, flat, outs)


def tables_kernel(neighbours, maps, rows, vt, idx, back, sent_v, slots, order, held, codes):
    value = rows[...]
    high = (value >> 9) * 2 + ((value >> 7) & 1)
    value = high * L + ((value >> 8) & 1) * 128 + (value & 127)
    idx[...] = value
    codes[...] = coded(value)
    held[...] = jnp.ones_like(held)
    me = lax.axis_index("sub")
    base = lax.rem(me, 2) * 64
    lane = lax.broadcasted_iota(i32, (1, 128), 1)
    for i in range(112):
        slots[i] = 0

    def two(half, carry):
        for n in (2 * half, 2 * half + 1):
            for j in range(SUBS):
                named = neighbours[j, n]
                none = named < 0
                step = ((named >> 2) - me) & 31
                other = named & 3
                sent = jnp.where(none, 7, maps[base + step])
                source = maps[base + 32 + step]
                at = ((sent - 1) & 7) * 16 + other * 3
                line = codes[n, j : j + 1, :]
                for t in range(3):
                    held[j, pl.ds(at + t, 1), :] = line[:, 128 * t : 128 * t + 128]
                slots[jnp.where(none, 112, source * 16 + other * 4 + j)] = n
                near = other * 8 + jnp.where(source == 0, (other ^ j) - 1, 2 + j)
                later = (source >> 1) * 32 + other * 8 + (source & 1) * 4 + j
                spot = jnp.where(source < 6, later, 96 + other * 4 + j)
                spot = jnp.where(none, -1, jnp.where(source < 2, near, spot))
                order[pl.ds(n * 4 + j, 1), :] = (lane == spot).astype(f32)
        return carry

    lax.fori_loop(0, NB // 2, two, 0)
    back[...] = held[:, 112:, :]
    sent_v[:, :12] = vt[...]
    sent_v[:, 12] = held[:, :K, :].astype(bf16)


def final_kernel(order, *refs):
    pieces, (out, out_self, total) = refs[:-3], refs[-3:]
    start = 0
    for chunk, count in enumerate(CHUNKS):
        own, r1, r2, r3 = pieces[4 * chunk : 4 * chunk + 4]
        total[start : start + count, :] = (
            own[...] + r1[...].astype(f32) + r2[...].astype(f32) + r3[...].astype(f32)
        )
        start += count
    total[start:, :] = jnp.zeros((128 - start, SHARE), f32)
    for s in range(SUBS):
        out_self[s : s + 1, :] = total[s * 8 + 6 : s * 8 + 7, :] * float(ROWS * 4) ** (-0.5)
    which = order[...].astype(bf16)
    rest = total[...]
    placed = None
    for _ in range(3):
        part = rest.astype(bf16)
        rest = rest - part.astype(f32)
        taken = jnp.dot(which, part, preferred_element_type=f32)
        placed = taken if placed is None else placed + taken
    for n in range(NB):
        out[n] = placed[4 * n : 4 * n + 4]


def share_shapes(count):
    return [jax.ShapeDtypeStruct((count, SHARE), f32 if s == 0 else bf16) for s in range(4)]


def row_exchange(shares):
    return [shares[0]] + [
        lax.ppermute(shares[s], "row", [(i, (i + s) % 4) for i in range(4)]) for s in (1, 2, 3)
    ]


def whole(shape):
    return pl.BlockSpec(shape, lambda *_: (0,) * len(shape))


def on_device(deflation, center, stiffness, coupling, neighbours, shared_rows):
    n_sub = lax.axis_size("sub")
    smem = pl.BlockSpec(memory_space=pltpu.SMEM)
    vt = jnp.transpose(deflation, (0, 2, 4, 3, 1, 5))
    vt = lax.optimization_barrier(vt)
    halo = (SUBS, 6, K, 128)
    below = lax.ppermute(vt[:, :, 1], "row", [(i, i + 1) for i in range(3)]).reshape(halo)
    above = lax.ppermute(vt[:, :, 0], "row", [(i + 1, i) for i in range(3)]).reshape(halo)

    maps = []
    for tables in ((TARGET_EVEN, SOURCE_EVEN), (TARGET_ODD, SOURCE_ODD)):
        for offsets in tables:
            line = [0] * 32
            for route, offset in enumerate(offsets):
                line[offset % n_sub] = route
            maps += line
    idx, back, sent_v, slots, order = call(
        tables_kernel,
        [
            jax.ShapeDtypeStruct((NB, SUBS, OV), i32),
            jax.ShapeDtypeStruct((SUBS, 16, 128), f32),
            jax.ShapeDtypeStruct((SUBS, TILES, K, 128), bf16),
            jax.ShapeDtypeStruct((128,), i32),
            jax.ShapeDtypeStruct((SUBS * NB, 128), f32),
        ],
        pltpu.PrefetchScalarGridSpec(
            num_scalar_prefetch=2,
            grid=(1,),
            in_specs=[whole((NB, SUBS, OV)), whole((SUBS, 12, K, 128))],
            out_specs=[
                whole((NB, SUBS, OV)),
                whole((SUBS, 16, 128)),
                whole((SUBS, TILES, K, 128)),
                smem,
                whole((SUBS * NB, 128)),
            ],
            scratch_shapes=[
                pltpu.VMEM((SUBS, 128, 128), f32),
                pltpu.VMEM((NB, SUBS, OV), f32),
            ],
        ),
        2 * 10**9,
        3 << 20,
    )(
        neighbours,
        jnp.array(maps, i32),
        jnp.transpose(shared_rows, (1, 0, 2)),
        vt.reshape(SUBS, 12, K, 128),
    )

    ring = lambda x, by: lax.ppermute(x, "sub", [(i, (i + by) % n_sub) for i in range(n_sub)])
    swap = lambda x: lax.ppermute(x, "sub", [(i, i ^ 1) for i in range(n_sub)])
    plus2, minus2 = ring(sent_v, -2), ring(sent_v, 2)
    other = swap(sent_v)

    coup = coupling.reshape(26, 9)
    v_spec = pl.BlockSpec((1, TILES, K, 128), lambda s, *_: (s, 0, 0, 0))
    halo_spec = pl.BlockSpec((1, 6, K, 128), lambda s, *_: (s, 0, 0, 0))
    a_spec = pl.BlockSpec((1, G, K, L), lambda s, *_: (s, 0, 0, 0))
    stiff_spec = pl.BlockSpec((1, 26, 2, 2, 128), lambda s, *_: (s, 0, 0, 0, 0))
    inner = call(
        inner_kernel,
        jax.ShapeDtypeStruct((SUBS, G, K, L), f32),
        pl.GridSpec(
            grid=(SUBS,),
            in_specs=[
                smem,
                v_spec,
                stiff_spec,
                pl.BlockSpec((1, 2, 2, 128), lambda s: (s, 0, 0, 0)),
            ],
            out_specs=a_spec,
        ),
        5 * 10**9,
        5 << 20,
    )(coup, sent_v, stiffness, center)

    found = call(
        early_kernel,
        jax.ShapeDtypeStruct((SUBS, K, 6 * OV), bf16),
        pl.GridSpec(
            grid=(SUBS,),
            in_specs=[v_spec, v_spec, pl.BlockSpec((1, 16, 128), lambda s: (s, 0, 0))],
            out_specs=pl.BlockSpec((1, K, 6 * OV), lambda s: (s, 0, 0)),
        ),
        5 * 10**9,
        5 << 20,
    )(sent_v, other, back)

    below, above, found = lax.optimization_barrier((below, above, found))
    applied = call(
        outer_kernel,
        jax.ShapeDtypeStruct((SUBS, G, K, L), bf16),
        pl.GridSpec(
            grid=(SUBS,),
            in_specs=[smem, a_spec, halo_spec, halo_spec, stiff_spec],
            out_specs=a_spec,
        ),
        3 * 10**9,
        6 << 20,
    )(coup, inner, below, above, stiffness)

    def take_rows(s, idx):
        return call(
            functools.partial(own_rows_kernel, s),
            jax.ShapeDtypeStruct((K, NB * OV), bf16),
            pl.GridSpec(
                grid=(1,),
                in_specs=[
                    pl.BlockSpec((1, G, K, L), lambda i: (s, 0, 0, 0)),
                    whole((NB, SUBS, OV)),
                ],
                out_specs=whole((K, NB * OV)),
            ),
            6 * 10**9,
            4 << 20,
        )(applied, idx)

    own_rows = [take_rows(s, idx) for s in range(HOLD)]
    idx, plus2, minus2, own_rows[HOLD - 1] = lax.optimization_barrier(
        (idx, plus2, minus2, own_rows[HOLD - 1])
    )
    own_rows += [take_rows(s, idx) for s in range(HOLD, SUBS)]
    far = lax.ppermute(
        jnp.where(lax.axis_index("sub") % 2 == 0, plus2, minus2),
        "sub",
        [(i, (i - 1) % n_sub if i % 2 == 0 else (i + 1) % n_sub) for i in range(n_sub)],
    )
    plus2x, minus2x = swap(plus2), swap(minus2)

    def row_spec(route, p, step, q):
        return pl.BlockSpec((K, OV), lambda i, t: (0, t[route * 16 + (p + step * i) * 4 + q]))

    share_specs = lambda n: [pl.BlockSpec((n, SHARE), lambda i, *_: (i, 0))] * 4
    scratch = lambda n: [pltpu.VMEM((n, K, 128), f32), pltpu.VMEM((n, K * K), f32)]
    near = [
        (route, p, 0, q)
        for p in range(SUBS)
        for route, q in [(0, p ^ 1), (0, p ^ 2)] + [(1, q) for q in range(SUBS)]
    ]
    near_shares = call(
        first_pairs_kernel,
        share_shapes(CHUNKS[0]),
        pltpu.PrefetchScalarGridSpec(
            num_scalar_prefetch=1,
            grid=(1,),
            in_specs=[
                whole((SUBS, K, 6 * OV)),
                whole((SUBS, G, K, L)),
                whole((SUBS, TILES, K, 128)),
            ]
            + [row_spec(*spot) for spot in near],
            out_specs=share_specs(32),
            scratch_shapes=scratch(32),
        ),
        3 * 10**9,
        8 << 20,
    )(slots, found, applied, sent_v, *[own_rows[spot[3]] for spot in near])

    blocks = [sent_v, other, plus2, minus2, plus2x, minus2x, far]
    pieces = []
    for routes in ((2, 3), (4, 5), (6,)):
        n = len(routes)
        rows = [
            (route, p, 4 // n, q) for p in range(4 // n) for route in routes for q in range(SUBS)
        ]
        earlier = near_shares if routes[0] == 2 else []
        skip = len(earlier) // 2
        shares = call(
            functools.partial(pairs_kernel, routes, len(earlier)),
            share_shapes(16 * (n + skip)),
            pltpu.PrefetchScalarGridSpec(
                num_scalar_prefetch=1,
                grid=(n,),
                in_specs=[pl.BlockSpec((4 // n, TILES, K, 128), lambda i, t: (i, 0, 0, 0))] * n
                + [row_spec(*spot) for spot in rows]
                + [pl.BlockSpec(memory_space=pl.ANY)] * len(earlier),
                out_specs=[pl.BlockSpec((16, SHARE), lambda i, t, skip=skip: (i + skip, 0))] * 4,
                scratch_shapes=scratch(16),
            ),
            n * 5 * 10**9,
            n * 5 << 20,
            {1 + n + 16 + s: s for s in range(len(earlier))},
        )(slots, *[blocks[o] for o in routes], *[own_rows[spot[3]] for spot in rows], *earlier)
        pieces += row_exchange(shares)

    pairs, selfs = call(
        final_kernel,
        [
            jax.ShapeDtypeStruct((NB, SUBS, SHARE), f32),
            jax.ShapeDtypeStruct((SUBS, SHARE), f32),
        ],
        pl.GridSpec(
            grid=(1,),
            in_specs=[whole((SUBS * NB, 128))]
            + [whole((count, SHARE)) for count in CHUNKS for _ in range(4)],
            out_specs=[whole((NB, SUBS, SHARE)), whole((SUBS, SHARE))],
            scratch_shapes=[pltpu.VMEM((128, SHARE), f32)],
        ),
        10**7,
        4 << 20,
    )(order, *pieces)
    return jnp.transpose(pairs, (1, 0, 2)), selfs


HOLD = 3


def solution(mesh):
    return jax.shard_map(
        on_device,
        mesh=mesh,
        in_specs=(
            P("sub", None, None, None, "row", None),
            P("sub", None, "row", None),
            P("sub", None, None, "row", None),
            P(),
            P("sub", None),
            P("sub", None, "row"),
        ),
        out_specs=(P("sub", None, "row"), P("sub", "row")),
        check_vma=False,
    )
```

```python
import functools

import jax
import jax.numpy as jnp
from jax import lax
from jax.experimental import pallas as pl
from jax.experimental.pallas import tpu as pltpu
from jax.sharding import PartitionSpec as P

f32, bf16, i32, i16 = jnp.float32, jnp.bfloat16, jnp.int32, jnp.int16
K, SUBS, NB, OV, ROWS = 96, 4, 26, 384, 1536
G, L = 6, 256
SHARE = K * K // 4
TILES = 13

SOURCE_EVEN = (0, 1, 2, -2, 3, -1, -3)
TARGET_EVEN = (0, 1, -2, 2, -1, 3, -3)
SOURCE_ODD = (0, -1, 2, -2, 1, -3, 3)
TARGET_ODD = (0, -1, -2, 2, -3, 1, 3)
CHUNKS = (32, 48, 32)


def call(kernel, out_shape, grid_spec, mib, flops, moved, aliases={}):
    return pl.pallas_call(
        kernel,
        out_shape=out_shape,
        grid_spec=grid_spec,
        input_output_aliases=aliases,
        compiler_params=pltpu.CompilerParams(vmem_limit_bytes=mib << 20),
        cost_estimate=pl.CostEstimate(flops=flops, bytes_accessed=moved, transcendentals=0),
    )


def nt_dot(a, b):
    return lax.dot_general(a, b, (((1,), (1,)), ((), ())), preferred_element_type=f32)


def put_shares(blocks, flat, outs):
    n = blocks.shape[0]
    lane = lax.broadcasted_iota(i32, (n, 128), 1)
    for a in range(K // 4):
        x0, x1, x2, x3 = (blocks[:, 4 * a + i, :] for i in range(4))
        x1, x2, x3 = pltpu.roll(x1, 96, 1), pltpu.roll(x2, 64, 1), pltpu.roll(x3, 32, 1)
        flat[:, 384 * a : 384 * a + 128] = jnp.where(lane < 96, x0, x1)
        flat[:, 384 * a + 128 : 384 * a + 256] = jnp.where(lane < 64, x1, x2)
        flat[:, 384 * a + 256 : 384 * a + 384] = jnp.where(lane < 32, x2, x3)
    row = lax.axis_index("row")
    for step in range(4):
        start = pl.multiple_of(lax.rem(row + step, 4) * SHARE, 128)
        outs[step][...] = flat[:, pl.ds(start, SHARE)].astype(outs[step].dtype)


def wide(ref, s, g):
    return jnp.concatenate([ref[s, 2 * g], ref[s, 2 * g + 1]], axis=1)


def offset_number(sx, sy, sz):
    flat = (sx + 1) * 9 + (sy + 1) * 3 + sz + 1
    return None if flat == 13 else flat - (flat > 13)


def band_tile(distance, coup, stiff, c, b, y, sy):
    weights = {}
    for x in range(2):
        for x_in in range(2):
            for sz in (-1, 0, 1):
                o = offset_number(x_in - x, sy, sz)
                if o is not None:
                    w = jnp.broadcast_to(stiff[0, o, x, y : y + 1, :], (16, 128))
                    weights[x, x_in, sz] = (w * coup[o, c * 3 + b]).astype(bf16)
    lines = [[], []]
    for t in range(8):
        on_band = {sz: distance == sz - 16 * t for sz in (-1, 0, 1)}
        for x_in in range(2):
            parts = []
            for x in range(2):
                block = jnp.zeros((16, 128), bf16)
                for sz in (-1, 0, 1):
                    if (x, x_in, sz) in weights:
                        block = jnp.where(on_band[sz], weights[x, x_in, sz], block)
                parts.append(block)
            lines[x_in].append(jnp.concatenate(parts, axis=1))
    return jnp.concatenate(lines[0] + lines[1], axis=0)


def bands():
    return (
        lax.broadcasted_iota(i32, (16, 128), 0) - lax.broadcasted_iota(i32, (16, 128), 1)
    ).astype(i16)


def inner_kernel(coup, v, stiff, center, out):
    on_band = bands()

    def component(c, carry):
        for y in range(2):
            mid = wide(v, 0, 2 * c + y)
            diag = jnp.concatenate([center[0, x, y : y + 1, :] for x in range(2)], axis=1)
            spots = [(y_in, b) for y_in in range(2) for b in range(3)]
            lhs = jnp.concatenate([wide(v, 0, 2 * b + y_in) for y_in, b in spots], axis=1)
            tiles = [band_tile(on_band, coup, stiff, c, b, y, y_in - y) for y_in, b in spots]
            total = jnp.dot(lhs, jnp.concatenate(tiles, axis=0), preferred_element_type=f32)
            out[0, 2 * c + y] = diag * mid.astype(f32) - total
        return carry

    lax.fori_loop(0, 3, component, 0)


def outer_kernel(coup, inner, below, above, stiff, out):
    on_band = bands()

    def component(c, carry):
        for y in range(2):
            lhs = jnp.concatenate([wide(above if y else below, 0, b) for b in range(3)], axis=1)
            tiles = [band_tile(on_band, coup, stiff, c, b, y, 2 * y - 1) for b in range(3)]
            total = jnp.dot(lhs, jnp.concatenate(tiles, axis=0), preferred_element_type=f32)
            out[0, 2 * c + y] = (inner[0, 2 * c + y] - total).astype(bf16)
        return carry

    lax.fori_loop(0, 3, component, 0)


def gather_columns(stacked, high, low):
    tiles = []
    for t in range(high.shape[1] // L):
        part = high[:, t * L : t * L + L]
        hot = jnp.where(
            lax.broadcasted_iota(i16, (L, L), 0) == low[:, t * L : t * L + L].astype(i16),
            bf16(1),
            bf16(0),
        )
        found = jnp.dot(stacked, hot, preferred_element_type=f32)
        out = found[0:K]
        for g in range(1, G):
            out = jnp.where(part == g, found[g * K : g * K + K], out)
        tiles.append(out.astype(bf16))
    return jnp.concatenate(tiles, axis=1)


def stack_groups(v, s):
    return jnp.concatenate([wide(v, s, g) for g in range(G)], axis=0)


def coded(rows):
    h = rows >> 7
    e = jnp.where(h >= 6, h - 6, h)
    value = 1.0 + (rows & 127).astype(f32) * (1.0 / 128)
    for i in range(1, 6):
        value = jnp.where(e >= i, value * 2, value)
    return jnp.where(h >= 6, -value, value)


def decoded(value):
    size = jnp.abs(value)
    h = jnp.where(value < 0, 6, 0)
    for i in range(1, 6):
        more = size >= 2
        h += more.astype(i32)
        size = jnp.where(more, size * 0.5, size)
    return h * 128 + ((size - 1.0) * 128).astype(i32)


def lines(held, first, count):
    return jnp.concatenate([held[first + t : first + t + 1] for t in range(count)], axis=1)


def gather_sent(v, s, route):
    held = decoded(v[s, 12, 16 * (route - 1) : 16 * route, :].astype(f32))
    rows = lines(held, 0, 12)
    return gather_columns(stack_groups(v, s), rows >> 8, rows & 255)


def own_rows_kernel(s, a, idx, out):
    stacked = a[0].reshape(G * K, L)

    def take(first, count):
        rows = jnp.concatenate([idx[first + t, s : s + 1, :] for t in range(count)], axis=1)
        at = pl.ds(pl.multiple_of(first * OV, 128), count * OV)
        out[:, at] = gather_columns(stacked, rows >> 8, rows & 255)

    def four_slots(t, carry):
        take(4 * t, 4)
        return carry

    lax.fori_loop(0, NB // 4, four_slots, 0)
    take(NB - 2, 2)


def early_kernel(v, v_other, back, out):
    p = pl.program_id(0)
    held = decoded(back[0])
    line = [lines(held, 3 * q, 3) for q in range(SUBS)]
    odd = p % 2 == 1
    swapped = [jnp.where(odd, line[a ^ 1], line[a]) for a in range(SUBS)]
    first = jnp.where(p < 2, swapped[1], swapped[3])
    second = jnp.where(p < 2, swapped[2], swapped[0])
    rows = jnp.concatenate([first, second], axis=1)
    out[0, :, : 2 * OV] = gather_columns(stack_groups(v, 0), rows >> 8, rows & 255)
    out[0, :, 2 * OV :] = gather_sent(v_other, 0, 1)


def first_pairs_kernel(slots, found, a, v, *refs):
    own_rows, outs, (blocks, flat) = refs[:24], refs[24:28], refs[28:]
    for p in range(SUBS):
        for j in range(6):
            blocks[p * 8 + j, :, :K] = nt_dot(
                own_rows[p * 6 + j][...], found[p, :, j * OV : j * OV + OV]
            )
        own = None
        for g in range(G):
            part = nt_dot(a[p, g], wide(v, p, g))
            own = part if own is None else own + part
        blocks[p * 8 + 6, :, :K] = own
        blocks[p * 8 + 7, :, :] = jnp.zeros((K, 128), f32)
    put_shares(blocks, flat, outs)


def pairs_kernel(routes, earlier, slots, *refs):
    n = len(routes)
    v, own_rows = refs[:n], refs[n : n + 16]
    refs = refs[n + 16 + earlier :]
    outs, (blocks, flat) = refs[:4], refs[4:]
    for p in range(4 // n):
        for r in range(n):
            found = gather_sent(v[r], p, routes[r])
            for q in range(SUBS):
                j = (p * n + r) * 4 + q
                blocks[j, :, :K] = nt_dot(own_rows[j][...], found[:, q * OV : q * OV + OV])
    put_shares(blocks, flat, outs)


def tables_kernel(
    neighbours, maps, rows, vt, idx, back, sent_v, low, up, slots, order, held, codes
):
    value = rows[...]
    high = (value >> 9) * 2 + ((value >> 7) & 1)
    value = high * L + ((value >> 8) & 1) * 128 + (value & 127)
    idx[...] = value
    codes[...] = coded(value)
    held[...] = jnp.ones_like(held)
    me = lax.axis_index("sub")
    base = lax.rem(me, 2) * 64
    lane = lax.broadcasted_iota(i32, (1, 128), 1)
    for i in range(112):
        slots[i] = 0

    def two(half, carry):
        for n in (2 * half, 2 * half + 1):
            for j in range(SUBS):
                named = neighbours[j, n]
                none = named < 0
                step = ((named >> 2) - me) & 31
                other = named & 3
                sent = jnp.where(none, 7, maps[base + step])
                source = maps[base + 32 + step]
                at = ((sent - 1) & 7) * 16 + other * 3
                line = codes[n, j : j + 1, :]
                for t in range(3):
                    held[j, pl.ds(at + t, 1), :] = line[:, 128 * t : 128 * t + 128]
                slots[jnp.where(none, 112, source * 16 + other * 4 + j)] = n
                near = other * 8 + jnp.where(source == 0, (other ^ j) - 1, 2 + j)
                later = jnp.where(source < 4, 32, 80) + other * 8 + (source & 1) * 4 + j
                spot = jnp.where(source < 6, later, 64 + other * 4 + j)
                spot = jnp.where(none, -1, jnp.where(source < 2, near, spot))
                order[pl.ds(n * 4 + j, 1), :] = (lane == spot).astype(f32)
        return carry

    lax.fori_loop(0, NB // 2, two, 0)
    back[...] = held[:, 112:, :]
    sent_v[:, :12] = vt[...]
    for c in range(3):
        low[:, 2 * c : 2 * c + 2] = vt[:, 4 * c : 4 * c + 2]
        up[:, 2 * c : 2 * c + 2] = vt[:, 4 * c + 2 : 4 * c + 4]
    sent_v[:, 12] = held[:, :K, :].astype(bf16)


def final_kernel(order, *refs):
    pieces, (out, out_self, total) = refs[:-3], refs[-3:]
    start = 0
    for chunk, count in enumerate(CHUNKS):
        own, r1, r2, r3 = pieces[4 * chunk : 4 * chunk + 4]
        total[start : start + count, :] = (
            own[...] + r1[...].astype(f32) + r2[...].astype(f32) + r3[...].astype(f32)
        )
        start += count
    total[start:, :] = jnp.zeros((128 - start, SHARE), f32)
    for s in range(SUBS):
        out_self[s : s + 1, :] = total[s * 8 + 6 : s * 8 + 7, :] * float(ROWS * 4) ** (-0.5)
    which = order[...].astype(bf16)
    rest = total[...]
    placed = None
    for _ in range(3):
        part = rest.astype(bf16)
        rest = rest - part.astype(f32)
        taken = jnp.dot(which, part, preferred_element_type=f32)
        placed = taken if placed is None else placed + taken
    for n in range(NB):
        out[n] = placed[4 * n : 4 * n + 4]


def share_shapes(count):
    return [jax.ShapeDtypeStruct((count, SHARE), f32 if s == 0 else bf16) for s in range(4)]


def row_exchange(shares):
    return [shares[0]] + [
        lax.ppermute(shares[s], "row", [(i, (i + s) % 4) for i in range(4)]) for s in (1, 2, 3)
    ]


def whole(shape):
    return pl.BlockSpec(shape, lambda *_: (0,) * len(shape))


def on_device(deflation, center, stiffness, coupling, neighbours, shared_rows):
    n_sub = lax.axis_size("sub")
    smem = pl.BlockSpec(memory_space=pltpu.SMEM)
    vt = jnp.transpose(deflation, (0, 2, 4, 3, 1, 5))
    maps = []
    for tables in ((TARGET_EVEN, SOURCE_EVEN), (TARGET_ODD, SOURCE_ODD)):
        for offsets in tables:
            line = [0] * 32
            for route, offset in enumerate(offsets):
                line[offset % n_sub] = route
            maps += line
    idx, back, sent_v, low, up, slots, order = call(
        tables_kernel,
        [
            jax.ShapeDtypeStruct((NB, SUBS, OV), i32),
            jax.ShapeDtypeStruct((SUBS, 16, 128), f32),
            jax.ShapeDtypeStruct((SUBS, TILES, K, 128), bf16),
            jax.ShapeDtypeStruct((SUBS, 6, K, 128), bf16),
            jax.ShapeDtypeStruct((SUBS, 6, K, 128), bf16),
            jax.ShapeDtypeStruct((128,), i32),
            jax.ShapeDtypeStruct((SUBS * NB, 128), f32),
        ],
        pltpu.PrefetchScalarGridSpec(
            num_scalar_prefetch=2,
            grid=(1,),
            in_specs=[whole((NB, SUBS, OV)), whole((SUBS, 12, K, 128))],
            out_specs=[
                whole((NB, SUBS, OV)),
                whole((SUBS, 16, 128)),
                whole((SUBS, TILES, K, 128)),
                whole((SUBS, 6, K, 128)),
                whole((SUBS, 6, K, 128)),
                smem,
                whole((SUBS * NB, 128)),
            ],
            scratch_shapes=[
                pltpu.VMEM((SUBS, 128, 128), f32),
                pltpu.VMEM((NB, SUBS, OV), f32),
            ],
        ),
        12,
        2 * 10**9,
        3 << 20,
    )(
        neighbours,
        jnp.array(maps, i32),
        jnp.transpose(shared_rows, (1, 0, 2)),
        vt.reshape(SUBS, 12, K, 128),
    )

    ring = lambda x, by: lax.ppermute(x, "sub", [(i, (i + by) % n_sub) for i in range(n_sub)])
    swap = lambda x: lax.ppermute(x, "sub", [(i, i ^ 1) for i in range(n_sub)])
    plus2, minus2 = ring(sent_v, -2), ring(sent_v, 2)
    below = lax.ppermute(up, "row", [(i, i + 1) for i in range(3)])
    above = lax.ppermute(low, "row", [(i + 1, i) for i in range(3)])
    other = swap(sent_v)

    coup = coupling.reshape(26, 9)
    v_spec = pl.BlockSpec((1, TILES, K, 128), lambda s, *_: (s, 0, 0, 0))
    halo_spec = pl.BlockSpec((1, 6, K, 128), lambda s, *_: (s, 0, 0, 0))
    a_spec = pl.BlockSpec((1, G, K, L), lambda s, *_: (s, 0, 0, 0))
    stiff_spec = pl.BlockSpec((1, 26, 2, 2, 128), lambda s, *_: (s, 0, 0, 0, 0))
    found = call(
        early_kernel,
        jax.ShapeDtypeStruct((SUBS, K, 6 * OV), bf16),
        pl.GridSpec(
            grid=(SUBS,),
            in_specs=[v_spec, v_spec, pl.BlockSpec((1, 16, 128), lambda s: (s, 0, 0))],
            out_specs=pl.BlockSpec((1, K, 6 * OV), lambda s: (s, 0, 0)),
        ),
        10,
        5 * 10**9,
        5 << 20,
    )(sent_v, other, back)

    stiffness, found = lax.optimization_barrier((stiffness, found))
    inner = call(
        inner_kernel,
        jax.ShapeDtypeStruct((SUBS, G, K, L), f32),
        pl.GridSpec(
            grid=(SUBS,),
            in_specs=[
                smem,
                v_spec,
                stiff_spec,
                pl.BlockSpec((1, 2, 2, 128), lambda s: (s, 0, 0, 0)),
            ],
            out_specs=a_spec,
        ),
        10,
        5 * 10**9,
        5 << 20,
    )(coup, sent_v, stiffness, center)

    below, above, inner = lax.optimization_barrier((below, above, inner))
    applied = call(
        outer_kernel,
        jax.ShapeDtypeStruct((SUBS, G, K, L), bf16),
        pl.GridSpec(
            grid=(SUBS,),
            in_specs=[smem, a_spec, halo_spec, halo_spec, stiff_spec],
            out_specs=a_spec,
        ),
        10,
        3 * 10**9,
        6 << 20,
    )(coup, inner, below, above, stiffness)

    def take_rows(s, idx):
        return call(
            functools.partial(own_rows_kernel, s),
            jax.ShapeDtypeStruct((K, NB * OV), bf16),
            pl.GridSpec(
                grid=(1,),
                in_specs=[
                    pl.BlockSpec((1, G, K, L), lambda i: (s, 0, 0, 0)),
                    whole((NB, SUBS, OV)),
                ],
                out_specs=whole((K, NB * OV)),
            ),
            12,
            6 * 10**9,
            4 << 20,
        )(applied, idx)

    own_rows = [take_rows(s, idx) for s in range(HOLD)]
    idx, plus2, minus2, own_rows[HOLD - 1] = lax.optimization_barrier(
        (idx, plus2, minus2, own_rows[HOLD - 1])
    )
    own_rows += [take_rows(s, idx) for s in range(HOLD, SUBS)]
    far = lax.ppermute(
        jnp.where(lax.axis_index("sub") % 2 == 0, plus2, minus2),
        "sub",
        [(i, (i - 1) % n_sub if i % 2 == 0 else (i + 1) % n_sub) for i in range(n_sub)],
    )
    plus2x, minus2x = swap(plus2), swap(minus2)

    def row_spec(route, p, step, q):
        return pl.BlockSpec((K, OV), lambda i, t: (0, t[route * 16 + (p + step * i) * 4 + q]))

    scratch = lambda n: [pltpu.VMEM((n, K, 128), f32), pltpu.VMEM((n, K * K), f32)]
    near = [
        (route, p, 0, q)
        for p in range(SUBS)
        for route, q in [(0, p ^ 1), (0, p ^ 2)] + [(1, q) for q in range(SUBS)]
    ]
    near_shares, plus2, minus2, plus2x, minus2x = lax.optimization_barrier((call(
        first_pairs_kernel,
        share_shapes(32),
        pltpu.PrefetchScalarGridSpec(
            num_scalar_prefetch=1,
            grid=(1,),
            in_specs=[
                whole((SUBS, K, 6 * OV)),
                whole((SUBS, G, K, L)),
                whole((SUBS, TILES, K, 128)),
            ]
            + [row_spec(*spot) for spot in near],
            out_specs=[pl.BlockSpec((32, SHARE), lambda i, *_: (i, 0))] * 4,
            scratch_shapes=scratch(32),
        ),
        24,
        3 * 10**9,
        8 << 20,
    )(slots, found, applied, sent_v, *[own_rows[spot[3]] for spot in near]), plus2, minus2, plus2x, minus2x))
    pieces = row_exchange(near_shares)

    blocks = [sent_v, other, plus2, minus2, plus2x, minus2x, far]
    def later_pairs(routes, total, earlier=()):
        n = len(routes)
        skip = total // 16 - n if earlier else 0
        rows = [
            (route, p, 4 // n, q) for p in range(4 // n) for route in routes for q in range(SUBS)
        ]
        return call(
            functools.partial(pairs_kernel, routes, len(earlier)),
            share_shapes(total),
            pltpu.PrefetchScalarGridSpec(
                num_scalar_prefetch=1,
                grid=(n,),
                in_specs=[pl.BlockSpec((4 // n, TILES, K, 128), lambda i, t: (i, 0, 0, 0))] * n
                + [row_spec(*spot) for spot in rows]
                + [pl.BlockSpec(memory_space=pl.ANY)] * len(earlier),
                out_specs=[pl.BlockSpec((16, SHARE), lambda i, t: (i + skip, 0))] * 4,
                scratch_shapes=scratch(16),
            ),
            18,
            n * 5 * 10**9,
            n * 5 << 20,
            {1 + n + 16 + s: s for s in range(len(earlier))},
        )(slots, *[blocks[o] for o in routes], *[own_rows[spot[3]] for spot in rows], *earlier)

    shares = later_pairs((6,), 48, later_pairs((2, 3), 48))
    shares, blocks[4], blocks[5] = lax.optimization_barrier((shares, blocks[4], blocks[5]))
    for shares in (list(shares), list(later_pairs((4, 5), 32))):
        for s in (1, 2, 3):
            shares[s], pieces[s - 4] = lax.optimization_barrier((shares[s], pieces[s - 4]))
        pieces += row_exchange(shares)

    pairs, selfs = call(
        final_kernel,
        [
            jax.ShapeDtypeStruct((NB, SUBS, SHARE), f32),
            jax.ShapeDtypeStruct((SUBS, SHARE), f32),
        ],
        pl.GridSpec(
            grid=(1,),
            in_specs=[whole((SUBS * NB, 128))]
            + [whole((count, SHARE)) for count in CHUNKS for _ in range(4)],
            out_specs=[whole((NB, SUBS, SHARE)), whole((SUBS, SHARE))],
            scratch_shapes=[pltpu.VMEM((128, SHARE), f32)],
        ),
        16,
        10**7,
        4 << 20,
    )(order, *pieces)
    return jnp.transpose(pairs, (1, 0, 2)), selfs


HOLD = 3


def solution(mesh):
    return jax.shard_map(
        on_device,
        mesh=mesh,
        in_specs=(
            P("sub", None, None, None, "row", None),
            P("sub", None, "row", None),
            P("sub", None, None, "row", None),
            P(),
            P("sub", None),
            P("sub", None, "row"),
        ),
        out_specs=(P("sub", None, "row"), P("sub", "row")),
        check_vma=False,
    )
```

```python
import functools

import jax
import jax.numpy as jnp
from jax import lax
from jax.experimental import pallas as pl
from jax.experimental.pallas import tpu as pltpu
from jax.sharding import PartitionSpec as P

f32, bf16, i32, i16 = jnp.float32, jnp.bfloat16, jnp.int32, jnp.int16
K, SUBS, NB, OV, ROWS = 96, 4, 26, 384, 1536
G, L = 6, 256
SHARE = K * K // 4
TILES = 13

SOURCE_EVEN = (0, 1, 2, -2, 3, -1, -3)
TARGET_EVEN = (0, 1, -2, 2, -1, 3, -3)
SOURCE_ODD = (0, -1, 2, -2, 1, -3, 3)
TARGET_ODD = (0, -1, -2, 2, -3, 1, 3)
CHUNKS = (32, 48, 32)


def call(kernel, out_shape, grid_spec, mib, flops, moved, aliases={}):
    return pl.pallas_call(
        kernel,
        out_shape=out_shape,
        grid_spec=grid_spec,
        input_output_aliases=aliases,
        compiler_params=pltpu.CompilerParams(vmem_limit_bytes=mib << 20),
        cost_estimate=pl.CostEstimate(flops=flops, bytes_accessed=moved, transcendentals=0),
    )


def nt_dot(a, b):
    return lax.dot_general(a, b, (((1,), (1,)), ((), ())), preferred_element_type=f32)


def put_shares(blocks, flat, outs):
    n = blocks.shape[0]
    lane = lax.broadcasted_iota(i32, (n, 128), 1)
    for a in range(K // 4):
        x0, x1, x2, x3 = (blocks[:, 4 * a + i, :] for i in range(4))
        x1, x2, x3 = pltpu.roll(x1, 96, 1), pltpu.roll(x2, 64, 1), pltpu.roll(x3, 32, 1)
        flat[:, 384 * a : 384 * a + 128] = jnp.where(lane < 96, x0, x1)
        flat[:, 384 * a + 128 : 384 * a + 256] = jnp.where(lane < 64, x1, x2)
        flat[:, 384 * a + 256 : 384 * a + 384] = jnp.where(lane < 32, x2, x3)
    row = lax.axis_index("row")
    for step in range(4):
        start = pl.multiple_of(lax.rem(row + step, 4) * SHARE, 128)
        outs[step][...] = flat[:, pl.ds(start, SHARE)].astype(outs[step].dtype)


def wide(ref, s, g):
    return jnp.concatenate([ref[s, 2 * g], ref[s, 2 * g + 1]], axis=1)


def offset_number(sx, sy, sz):
    flat = (sx + 1) * 9 + (sy + 1) * 3 + sz + 1
    return None if flat == 13 else flat - (flat > 13)


def band_tile(distance, coup, stiff, c, b, y, sy):
    weights = {}
    for x in range(2):
        for x_in in range(2):
            for sz in (-1, 0, 1):
                o = offset_number(x_in - x, sy, sz)
                if o is not None:
                    w = jnp.broadcast_to(stiff[0, o, x, y : y + 1, :], (16, 128))
                    weights[x, x_in, sz] = (w * coup[o, c * 3 + b]).astype(bf16)
    lines = [[], []]
    for t in range(8):
        on_band = {sz: distance == sz - 16 * t for sz in (-1, 0, 1)}
        for x_in in range(2):
            parts = []
            for x in range(2):
                block = jnp.zeros((16, 128), bf16)
                for sz in (-1, 0, 1):
                    if (x, x_in, sz) in weights:
                        block = jnp.where(on_band[sz], weights[x, x_in, sz], block)
                parts.append(block)
            lines[x_in].append(jnp.concatenate(parts, axis=1))
    return jnp.concatenate(lines[0] + lines[1], axis=0)


def bands():
    return (
        lax.broadcasted_iota(i32, (16, 128), 0) - lax.broadcasted_iota(i32, (16, 128), 1)
    ).astype(i16)


def inner_kernel(coup, v, stiff, center, out):
    on_band = bands()

    def component(c, carry):
        for y in range(2):
            mid = wide(v, 0, 2 * c + y)
            diag = jnp.concatenate([center[0, x, y : y + 1, :] for x in range(2)], axis=1)
            spots = [(y_in, b) for y_in in range(2) for b in range(3)]
            lhs = jnp.concatenate([wide(v, 0, 2 * b + y_in) for y_in, b in spots], axis=1)
            tiles = [band_tile(on_band, coup, stiff, c, b, y, y_in - y) for y_in, b in spots]
            total = jnp.dot(lhs, jnp.concatenate(tiles, axis=0), preferred_element_type=f32)
            out[0, 2 * c + y] = diag * mid.astype(f32) - total
        return carry

    lax.fori_loop(0, 3, component, 0)


def outer_kernel(coup, inner, below, above, stiff, out):
    on_band = bands()

    def component(c, carry):
        for y in range(2):
            lhs = jnp.concatenate([wide(above if y else below, 0, b) for b in range(3)], axis=1)
            tiles = [band_tile(on_band, coup, stiff, c, b, y, 2 * y - 1) for b in range(3)]
            total = jnp.dot(lhs, jnp.concatenate(tiles, axis=0), preferred_element_type=f32)
            out[0, 2 * c + y] = (inner[0, 2 * c + y] - total).astype(bf16)
        return carry

    lax.fori_loop(0, 3, component, 0)


def gather_columns(stacked, high, low):
    tiles = []
    for t in range(high.shape[1] // L):
        part = high[:, t * L : t * L + L]
        hot = jnp.where(
            lax.broadcasted_iota(i16, (L, L), 0) == low[:, t * L : t * L + L].astype(i16),
            bf16(1),
            bf16(0),
        )
        found = jnp.dot(stacked, hot, preferred_element_type=f32)
        out = found[0:K]
        for g in range(1, G):
            out = jnp.where(part == g, found[g * K : g * K + K], out)
        tiles.append(out.astype(bf16))
    return jnp.concatenate(tiles, axis=1)


def stack_groups(v, s):
    return jnp.concatenate([wide(v, s, g) for g in range(G)], axis=0)


def coded(rows):
    h = rows >> 7
    e = jnp.where(h >= 6, h - 6, h)
    value = 1.0 + (rows & 127).astype(f32) * (1.0 / 128)
    for i in range(1, 6):
        value = jnp.where(e >= i, value * 2, value)
    return jnp.where(h >= 6, -value, value)


def decoded(value):
    size = jnp.abs(value)
    h = jnp.where(value < 0, 6, 0)
    for i in range(1, 6):
        more = size >= 2
        h += more.astype(i32)
        size = jnp.where(more, size * 0.5, size)
    return h * 128 + ((size - 1.0) * 128).astype(i32)


def lines(held, first, count):
    return jnp.concatenate([held[first + t : first + t + 1] for t in range(count)], axis=1)


def gather_sent(v, s, route):
    held = decoded(v[s, 12, 16 * (route - 1) : 16 * route, :].astype(f32))
    rows = lines(held, 0, 12)
    return gather_columns(stack_groups(v, s), rows >> 8, rows & 255)


def own_rows_kernel(s, a, idx, out):
    stacked = a[0].reshape(G * K, L)

    def take(first, count):
        rows = jnp.concatenate([idx[first + t, s : s + 1, :] for t in range(count)], axis=1)
        at = pl.ds(pl.multiple_of(first * OV, 128), count * OV)
        out[:, at] = gather_columns(stacked, rows >> 8, rows & 255)

    def four_slots(t, carry):
        take(4 * t, 4)
        return carry

    lax.fori_loop(0, NB // 4, four_slots, 0)
    take(NB - 2, 2)


def early_kernel(v, v_other, back, out):
    p = pl.program_id(0)
    held = decoded(back[0])
    line = [lines(held, 3 * q, 3) for q in range(SUBS)]
    odd = p % 2 == 1
    swapped = [jnp.where(odd, line[a ^ 1], line[a]) for a in range(SUBS)]
    first = jnp.where(p < 2, swapped[1], swapped[3])
    second = jnp.where(p < 2, swapped[2], swapped[0])
    rows = jnp.concatenate([first, second], axis=1)
    out[0, :, : 2 * OV] = gather_columns(stack_groups(v, 0), rows >> 8, rows & 255)
    out[0, :, 2 * OV :] = gather_sent(v_other, 0, 1)


def first_pairs_kernel(slots, found, a, v, *refs):
    own_rows, outs, (blocks, flat) = refs[:24], refs[24:28], refs[28:]
    for p in range(SUBS):
        for j in range(6):
            blocks[p * 8 + j, :, :K] = nt_dot(
                own_rows[p * 6 + j][...], found[p, :, j * OV : j * OV + OV]
            )
        own = None
        for g in range(G):
            part = nt_dot(a[p, g], wide(v, p, g))
            own = part if own is None else own + part
        blocks[p * 8 + 6, :, :K] = own
        blocks[p * 8 + 7, :, :] = jnp.zeros((K, 128), f32)
    put_shares(blocks, flat, outs)


def pairs_kernel(routes, earlier, slots, *refs):
    n = len(routes)
    v, own_rows = refs[:n], refs[n : n + 16]
    refs = refs[n + 16 + earlier :]
    outs, (blocks, flat) = refs[:4], refs[4:]
    for p in range(4 // n):
        for r in range(n):
            found = gather_sent(v[r], p, routes[r])
            for q in range(SUBS):
                j = (p * n + r) * 4 + q
                blocks[j, :, :K] = nt_dot(own_rows[j][...], found[:, q * OV : q * OV + OV])
    put_shares(blocks, flat, outs)


def tables_kernel(
    neighbours, maps, rows, vt, idx, back, sent_v, low, up, slots, order, held, codes
):
    value = rows[...]
    high = (value >> 9) * 2 + ((value >> 7) & 1)
    value = high * L + ((value >> 8) & 1) * 128 + (value & 127)
    idx[...] = value
    codes[...] = coded(value)
    held[...] = jnp.ones_like(held)
    me = lax.axis_index("sub")
    base = lax.rem(me, 2) * 64
    lane = lax.broadcasted_iota(i32, (1, 128), 1)
    for i in range(112):
        slots[i] = 0

    def two(half, carry):
        for n in (2 * half, 2 * half + 1):
            for j in range(SUBS):
                named = neighbours[j, n]
                none = named < 0
                step = ((named >> 2) - me) & 31
                other = named & 3
                sent = jnp.where(none, 7, maps[base + step])
                source = maps[base + 32 + step]
                at = ((sent - 1) & 7) * 16 + other * 3
                line = codes[n, j : j + 1, :]
                for t in range(3):
                    held[j, pl.ds(at + t, 1), :] = line[:, 128 * t : 128 * t + 128]
                slots[jnp.where(none, 112, source * 16 + other * 4 + j)] = n
                near = other * 8 + jnp.where(source == 0, (other ^ j) - 1, 2 + j)
                later = jnp.where(source < 4, 32, 80) + other * 8 + (source & 1) * 4 + j
                spot = jnp.where(source < 6, later, 64 + other * 4 + j)
                spot = jnp.where(none, -1, jnp.where(source < 2, near, spot))
                order[pl.ds(n * 4 + j, 1), :] = (lane == spot).astype(f32)
        return carry

    lax.fori_loop(0, NB // 2, two, 0)
    back[...] = held[:, 112:, :]
    sent_v[:, :12] = vt[...]
    for c in range(3):
        low[:, 2 * c : 2 * c + 2] = vt[:, 4 * c : 4 * c + 2]
        up[:, 2 * c : 2 * c + 2] = vt[:, 4 * c + 2 : 4 * c + 4]
    sent_v[:, 12] = held[:, :K, :].astype(bf16)


def final_kernel(order, *refs):
    pieces, (out, out_self, total) = refs[:-3], refs[-3:]
    start = 0
    for chunk, count in enumerate(CHUNKS):
        own, r1, r2, r3 = pieces[4 * chunk : 4 * chunk + 4]
        total[start : start + count, :] = (
            own[...] + r1[...].astype(f32) + r2[...].astype(f32) + r3[...].astype(f32)
        )
        start += count
    total[start:, :] = jnp.zeros((128 - start, SHARE), f32)
    for s in range(SUBS):
        out_self[s : s + 1, :] = total[s * 8 + 6 : s * 8 + 7, :] * float(ROWS * 4) ** (-0.5)
    which = order[...].astype(bf16)
    rest = total[...]
    placed = None
    for _ in range(3):
        part = rest.astype(bf16)
        rest = rest - part.astype(f32)
        taken = jnp.dot(which, part, preferred_element_type=f32)
        placed = taken if placed is None else placed + taken
    for n in range(NB):
        out[n] = placed[4 * n : 4 * n + 4]


def share_shapes(count):
    return [jax.ShapeDtypeStruct((count, SHARE), f32 if s == 0 else bf16) for s in range(4)]


def row_exchange(shares):
    return [shares[0]] + [
        lax.ppermute(shares[s], "row", [(i, (i + s) % 4) for i in range(4)]) for s in (1, 2, 3)
    ]


def whole(shape):
    return pl.BlockSpec(shape, lambda *_: (0,) * len(shape))


def on_device(deflation, center, stiffness, coupling, neighbours, shared_rows):
    n_sub = lax.axis_size("sub")
    smem = pl.BlockSpec(memory_space=pltpu.SMEM)
    vt = jnp.transpose(deflation, (0, 2, 4, 3, 1, 5))
    maps = []
    for tables in ((TARGET_EVEN, SOURCE_EVEN), (TARGET_ODD, SOURCE_ODD)):
        for offsets in tables:
            line = [0] * 32
            for route, offset in enumerate(offsets):
                line[offset % n_sub] = route
            maps += line
    idx, back, sent_v, low, up, slots, order = call(
        tables_kernel,
        [
            jax.ShapeDtypeStruct((NB, SUBS, OV), i32),
            jax.ShapeDtypeStruct((SUBS, 16, 128), f32),
            jax.ShapeDtypeStruct((SUBS, TILES, K, 128), bf16),
            jax.ShapeDtypeStruct((SUBS, 6, K, 128), bf16),
            jax.ShapeDtypeStruct((SUBS, 6, K, 128), bf16),
            jax.ShapeDtypeStruct((128,), i32),
            jax.ShapeDtypeStruct((SUBS * NB, 128), f32),
        ],
        pltpu.PrefetchScalarGridSpec(
            num_scalar_prefetch=2,
            grid=(1,),
            in_specs=[whole((NB, SUBS, OV)), whole((SUBS, 12, K, 128))],
            out_specs=[
                whole((NB, SUBS, OV)),
                whole((SUBS, 16, 128)),
                whole((SUBS, TILES, K, 128)),
                whole((SUBS, 6, K, 128)),
                whole((SUBS, 6, K, 128)),
                smem,
                whole((SUBS * NB, 128)),
            ],
            scratch_shapes=[
                pltpu.VMEM((SUBS, 128, 128), f32),
                pltpu.VMEM((NB, SUBS, OV), f32),
            ],
        ),
        12,
        2 * 10**9,
        3 << 20,
    )(
        neighbours,
        jnp.array(maps, i32),
        jnp.transpose(shared_rows, (1, 0, 2)),
        vt.reshape(SUBS, 12, K, 128),
    )

    ring = lambda x, by: lax.ppermute(x, "sub", [(i, (i + by) % n_sub) for i in range(n_sub)])
    swap = lambda x: lax.ppermute(x, "sub", [(i, i ^ 1) for i in range(n_sub)])
    plus2, minus2 = ring(sent_v, -2), ring(sent_v, 2)
    below = lax.ppermute(up, "row", [(i, i + 1) for i in range(3)])
    above = lax.ppermute(low, "row", [(i + 1, i) for i in range(3)])
    other = swap(sent_v)

    coup = coupling.reshape(26, 9)
    v_spec = pl.BlockSpec((1, TILES, K, 128), lambda s, *_: (s, 0, 0, 0))
    halo_spec = pl.BlockSpec((1, 6, K, 128), lambda s, *_: (s, 0, 0, 0))
    a_spec = pl.BlockSpec((1, G, K, L), lambda s, *_: (s, 0, 0, 0))
    stiff_spec = pl.BlockSpec((1, 26, 2, 2, 128), lambda s, *_: (s, 0, 0, 0, 0))
    found = call(
        early_kernel,
        jax.ShapeDtypeStruct((SUBS, K, 6 * OV), bf16),
        pl.GridSpec(
            grid=(SUBS,),
            in_specs=[v_spec, v_spec, pl.BlockSpec((1, 16, 128), lambda s: (s, 0, 0))],
            out_specs=pl.BlockSpec((1, K, 6 * OV), lambda s: (s, 0, 0)),
        ),
        10,
        10**8,
        1 << 18,
    )(sent_v, other, back)

    stiffness, found = lax.optimization_barrier((stiffness, found))
    inner = call(
        inner_kernel,
        jax.ShapeDtypeStruct((SUBS, G, K, L), f32),
        pl.GridSpec(
            grid=(SUBS,),
            in_specs=[
                smem,
                v_spec,
                stiff_spec,
                pl.BlockSpec((1, 2, 2, 128), lambda s: (s, 0, 0, 0)),
            ],
            out_specs=a_spec,
        ),
        10,
        10**8,
        1 << 18,
    )(coup, sent_v, stiffness, center)

    below, above, inner = lax.optimization_barrier((below, above, inner))
    applied = call(
        outer_kernel,
        jax.ShapeDtypeStruct((SUBS, G, K, L), bf16),
        pl.GridSpec(
            grid=(SUBS,),
            in_specs=[smem, a_spec, halo_spec, halo_spec, stiff_spec],
            out_specs=a_spec,
        ),
        10,
        3 * 10**9,
        6 << 20,
    )(coup, inner, below, above, stiffness)

    def take_rows(s, idx):
        return call(
            functools.partial(own_rows_kernel, s),
            jax.ShapeDtypeStruct((K, NB * OV), bf16),
            pl.GridSpec(
                grid=(1,),
                in_specs=[
                    pl.BlockSpec((1, G, K, L), lambda i: (s, 0, 0, 0)),
                    whole((NB, SUBS, OV)),
                ],
                out_specs=whole((K, NB * OV)),
            ),
            12,
            6 * 10**9,
            4 << 20,
        )(applied, idx)

    own_rows = [take_rows(s, idx) for s in range(HOLD)]
    idx, plus2, minus2, own_rows[HOLD - 1] = lax.optimization_barrier(
        (idx, plus2, minus2, own_rows[HOLD - 1])
    )
    own_rows += [take_rows(s, idx) for s in range(HOLD, SUBS)]
    far = lax.ppermute(
        jnp.where(lax.axis_index("sub") % 2 == 0, plus2, minus2),
        "sub",
        [(i, (i - 1) % n_sub if i % 2 == 0 else (i + 1) % n_sub) for i in range(n_sub)],
    )
    plus2x, minus2x = swap(plus2), swap(minus2)

    def row_spec(route, p, step, q):
        return pl.BlockSpec((K, OV), lambda i, t: (0, t[route * 16 + (p + step * i) * 4 + q]))

    scratch = lambda n: [pltpu.VMEM((n, K, 128), f32), pltpu.VMEM((n, K * K), f32)]
    near = [
        (route, p, 0, q)
        for p in range(SUBS)
        for route, q in [(0, p ^ 1), (0, p ^ 2)] + [(1, q) for q in range(SUBS)]
    ]
    near_shares, plus2, minus2, plus2x, minus2x = lax.optimization_barrier((call(
        first_pairs_kernel,
        share_shapes(32),
        pltpu.PrefetchScalarGridSpec(
            num_scalar_prefetch=1,
            grid=(1,),
            in_specs=[
                whole((SUBS, K, 6 * OV)),
                whole((SUBS, G, K, L)),
                whole((SUBS, TILES, K, 128)),
            ]
            + [row_spec(*spot) for spot in near],
            out_specs=[pl.BlockSpec((32, SHARE), lambda i, *_: (i, 0))] * 4,
            scratch_shapes=scratch(32),
        ),
        24,
        3 * 10**9,
        8 << 20,
    )(slots, found, applied, sent_v, *[own_rows[spot[3]] for spot in near]), plus2, minus2, plus2x, minus2x))
    pieces = row_exchange(near_shares)

    blocks = [sent_v, other, plus2, minus2, plus2x, minus2x, far]
    def later_pairs(routes, total, earlier=()):
        n = len(routes)
        skip = total // 16 - n if earlier else 0
        rows = [
            (route, p, 4 // n, q) for p in range(4 // n) for route in routes for q in range(SUBS)
        ]
        return call(
            functools.partial(pairs_kernel, routes, len(earlier)),
            share_shapes(total),
            pltpu.PrefetchScalarGridSpec(
                num_scalar_prefetch=1,
                grid=(n,),
                in_specs=[pl.BlockSpec((4 // n, TILES, K, 128), lambda i, t: (i, 0, 0, 0))] * n
                + [row_spec(*spot) for spot in rows]
                + [pl.BlockSpec(memory_space=pl.ANY)] * len(earlier),
                out_specs=[pl.BlockSpec((16, SHARE), lambda i, t: (i + skip, 0))] * 4,
                scratch_shapes=scratch(16),
            ),
            18,
            n * 5 * 10**9,
            n * 5 << 20,
            {1 + n + 16 + s: s for s in range(len(earlier))},
        )(slots, *[blocks[o] for o in routes], *[own_rows[spot[3]] for spot in rows], *earlier)

    shares = later_pairs((6,), 48, later_pairs((2, 3), 48))
    shares, blocks[4], blocks[5] = lax.optimization_barrier((shares, blocks[4], blocks[5]))
    for shares in (list(shares), list(later_pairs((4, 5), 32))):
        for s in (1, 2, 3):
            shares[s], pieces[s - 4] = lax.optimization_barrier((shares[s], pieces[s - 4]))
        pieces += row_exchange(shares)

    pairs, selfs = call(
        final_kernel,
        [
            jax.ShapeDtypeStruct((NB, SUBS, SHARE), f32),
            jax.ShapeDtypeStruct((SUBS, SHARE), f32),
        ],
        pl.GridSpec(
            grid=(1,),
            in_specs=[whole((SUBS * NB, 128))]
            + [whole((count, SHARE)) for count in CHUNKS for _ in range(4)],
            out_specs=[whole((NB, SUBS, SHARE)), whole((SUBS, SHARE))],
            scratch_shapes=[pltpu.VMEM((128, SHARE), f32)],
        ),
        16,
        10**7,
        4 << 20,
    )(order, *pieces)
    return jnp.transpose(pairs, (1, 0, 2)), selfs


HOLD = 3


def solution(mesh):
    return jax.shard_map(
        on_device,
        mesh=mesh,
        in_specs=(
            P("sub", None, None, None, "row", None),
            P("sub", None, "row", None),
            P("sub", None, None, "row", None),
            P(),
            P("sub", None),
            P("sub", None, "row"),
        ),
        out_specs=(P("sub", None, "row"), P("sub", "row")),
        check_vma=False,
    )
```
